32 devices in a mesh: parts: 2 (over x), row: 4 (over y, core), col: 4 (over z).
Axes of the slice: x: 2, y: 2, z: 4, core: 2. Of those that a mesh axis runs over, the one named last changes fastest.
Arguments:
- object_field: float32 [2, 2048, 2048], P(None, ('parts', 'row'), 'col'), parts along dimension 1, may hold values from -4 to 4
- probe_field: float32 [2, 128, 128], replicated, may hold values from -4 to 4
- amplitudes: float32 [4, 4, 24, 128, 128], P('row', 'col', 'parts'), parts along dimension 2, may hold values from 0.1 to 3
- positions: int32 [4, 4, 4, 12], P('row', 'col', 'parts'), parts along dimension 2, may hold values from 0 to 2047, as said below
- counts: int32 [8, 4], P(('parts', 'row'), 'col'), parts along dimension 0, may hold values from 1 to 12, 32 in all within a row
Outputs:
- object_out: float32 [2, 2048, 2048], P(None, ('parts', 'row'), 'col'), parts along dimension 1
- probe_out: float32 [4, 128, 128], P('parts'), parts along dimension 0
The draws below stay inside these ranges and needn't reach their ends.
There are 2 independent parts, one for each index of `parts`. The reference program is written for one: setup_inputs(seed, part) draws one part's arguments, and reference() takes and returns one part's arrays. A program takes and returns all parts, laid end to end along the dimension named above; an argument that names none is the same for every part. Nothing has to cross between parts.
Inputs may be any that keep to these rules, and one draw needn't show every extreme that they name: positions[a, b, 0, s] lies in a * 256 to (a + 1) * 256 - 1 and positions[a, b, 1, s] in b * 512 to (b + 1) * 512 - 1: every slot's centre lies in its own tile; centres sit on a grid of pitch 64 plus a jitter of 0 to 63 pixels along each dimension; slot 0 of tile (0, 0) is centred at (0, 0) and the last slot of the last tile at (1023, 2047). Slots 0 to counts[a, b] - 1 of tile (a, b) are recorded, the rest are to be ignored; each row of tiles holds 64 recorded patterns.
All inputs are finite; a program needn't handle non-finite values. No bound on the sum of `counts` on one device may be relied on, other than what follows from the above.
Results may differ from the reference program's by a relative error of at most 0.0003.
Values sent between devices are 32-bit elements; how exact they have to be, the bound alone decides.
A program may use at most 64 MiB of HBM per device.

```python
import math
import jax
import jax.numpy as jnp
import numpy as np
from jax import lax

PS = 128
TR = 256
TC = 512
SLOTS = 12
ITERS = 2
HALF = 64
NR = 1024
NC = 2048
TOTAL_POS = 128
N_ROW = 4
N_COL = 4


def draw_positions(key, part):
    key = jax.random.fold_in(key, 7)
    key_cell, key_row, key_col = jax.random.split(key, 3)
    across = TC // HALF
    cells = TR // HALF * across
    offset = jax.random.randint(key_cell, (N_ROW, N_COL, 1), 0, cells)
    slot = jnp.arange(SLOTS, dtype=jnp.int32)[None, None, :]
    cell = (slot + offset) % cells
    jitter_row = jax.random.randint(key_row, (N_ROW, N_COL, SLOTS), 0, HALF)
    jitter_col = jax.random.randint(key_col, (N_ROW, N_COL, SLOTS), 0, HALF)
    tile_row = jnp.arange(N_ROW, dtype=jnp.int32)[:, None, None] * TR
    tile_col = jnp.arange(N_COL, dtype=jnp.int32)[None, :, None] * TC
    centre_row = tile_row + cell // across * HALF + jitter_row
    centre_col = tile_col + cell % across * HALF + jitter_col
    centre_row = centre_row.at[0, 0, 0].set(0)
    centre_col = centre_col.at[0, 0, 0].set(0)
    centre_row = centre_row.at[N_ROW - 1, N_COL - 1, SLOTS - 1].set(NR - 1)
    centre_col = centre_col.at[N_ROW - 1, N_COL - 1, SLOTS - 1].set(NC - 1)
    return jnp.stack([centre_row, centre_col], axis=2).astype(jnp.int32)


def block_levels(rng, shape, cuts, least, top_value):
    def one(position, parts):
        heights = jax.random.uniform(jax.random.fold_in(jax.random.fold_in(rng, 6), position), (parts,), jnp.float32, least / len(cuts), top_value / len(cuts))
        return jnp.repeat(jnp.exp(heights), shape[position] // parts).reshape((-1,) + (1,) * (len(shape) - position - 1))

    loudness = one(*cuts[0])
    for cut in cuts[1:]:
        loudness = loudness * one(*cut)
    return loudness


def split_up(count, total, most, slope):
    loads = [(1 << 20) // math.isqrt(rank ** slope) + 1 for rank in range(2, count + 1)]
    spare, given = total - most - (count - 1), [1] * (count - 1)
    while spare > 0:
        candidates = [i for i in range(count - 1) if given[i] < most]
        mass, budget = sum([loads[i] for i in candidates]), spare
        for i in candidates:
            more = min(most - given[i], max(1, budget * loads[i] // mass), spare)
            given[i] = given[i] + more
            spare = spare - more
    return np.array([most] + given)


def uneven(stream_key, number_of, total, limit, slope):
    if number_of == 2:
        one = jax.random.randint(stream_key, (), max(1, total - limit), min(limit, total - 1) + 1)
        return jnp.stack([one, total - one])
    tallies = jnp.asarray(split_up(number_of, total, limit, slope), jnp.int32)
    pairs = (number_of - 1) // 2
    giver, taker = tallies[1:1 + 2 * pairs:2], tallies[2:2 + 2 * pairs:2]
    slack = jnp.minimum(giver - 1, limit - taker)
    passed = jax.random.randint(jax.random.fold_in(stream_key, 1), (pairs,), 0, 1 << 20) % (slack + 1)
    tallies = tallies.at[1:1 + 2 * pairs:2].set(giver - passed).at[2:2 + 2 * pairs:2].set(taker + passed)
    return tallies[jax.random.permutation(jax.random.fold_in(stream_key, 2), number_of)]


def noise(stream_key, extent, scale, reach, cuts=(), kind=jnp.bfloat16):
    level = block_levels(stream_key, extent, cuts, -0.22, 0.18) if cuts else 1.0
    values = jax.random.normal(stream_key, extent, jnp.float32) * scale * level
    return jnp.minimum(jnp.maximum(values, -reach), reach).astype(kind)


def setup_inputs(seed: int = 0, part: int = 0) -> dict:
    arg_keys = jax.random.split(jax.random.key(seed), 6)
    part_splits = jax.random.split(jax.random.fold_in(arg_keys[5], part), 6)
    return {
        "object_field": noise(part_splits[0], (2, NR, NC), 0.7, 4.0, ((1, 4), (2, 4)), jnp.float32),
        "probe_field": noise(arg_keys[1], (2, PS, PS), 0.7, 4.0, (), jnp.float32),
        "amplitudes": jnp.clip(jnp.exp(math.log(3.0) - 3.4011974 * jax.random.uniform(part_splits[2], (N_ROW, N_COL, SLOTS, PS, PS), jnp.float32) ** block_levels(part_splits[2], (N_ROW, N_COL, SLOTS, PS, PS), ((0, 4), (1, 4)), -0.2, 0.2)), 0.1, 3.0),
        "positions": draw_positions(jax.random.fold_in(jax.random.fold_in(arg_keys[5], part), 71), part),
        "counts": jax.vmap(lambda own: uneven(own, N_COL, N_COL * (2 * SLOTS // 3), SLOTS, 2))(jax.random.split(part_splits[4], N_ROW)).reshape((N_ROW, N_COL)).astype(jnp.int32),
    }


step_object = 0.25
step_probe = 0.5
floor_amp = 0.5


def residual_wave(patches, probe_field, amplitude, usable):
    object_real = patches[:, 0]
    object_imag = patches[:, 1]
    probe_real = probe_field[0]
    probe_imag = probe_field[1]
    exit_real = probe_real * object_real - probe_imag * object_imag
    exit_imag = probe_real * object_imag + probe_imag * object_real
    farfield = jnp.fft.fft2(lax.complex(exit_real, exit_imag), norm="ortho")
    modulus = jnp.abs(farfield)
    keeping = 1.0 - amplitude / jnp.maximum(modulus, floor_amp)
    change = jnp.fft.ifft2(farfield * keeping, norm="ortho")
    change_real = jnp.real(change) * usable[:, None, None]
    change_imag = jnp.imag(change) * usable[:, None, None]
    return change_real, change_imag


def reference(object_field, probe_field, amplitudes, positions, counts):
    tiles = N_ROW * N_COL
    centres = positions.reshape(tiles, 2, SLOTS).astype(jnp.int32)
    measured = amplitudes.reshape(tiles, SLOTS, PS, PS)
    totals = counts.reshape(tiles).astype(jnp.int32)
    zero_index = jnp.zeros((), jnp.int32)
    for iteration in range(ITERS):
        padded = jnp.pad(object_field, ((0, 0), (HALF, HALF), (HALF, HALF)))

        def per_tile(carry, inputs):
            grad_padded, grad_probe = carry
            centre, amplitude, total = inputs
            usable = (jnp.arange(SLOTS, dtype=jnp.int32) < total).astype(jnp.float32)

            def window(row_at, col_at):
                return lax.dynamic_slice(padded, (zero_index, row_at, col_at), (2, PS, PS))

            patches = jax.vmap(window)(centre[0], centre[1])
            change_real, change_imag = residual_wave(patches, probe_field, amplitude, usable)
            object_real = patches[:, 0]
            object_imag = patches[:, 1]
            probe_part = jnp.stack([jnp.sum(object_real * change_real + object_imag * change_imag, axis=0),
                                    jnp.sum(object_real * change_imag - object_imag * change_real, axis=0)])
            grad_real = probe_field[0] * change_real + probe_field[1] * change_imag
            grad_imag = probe_field[0] * change_imag - probe_field[1] * change_real
            pieces = jnp.stack([grad_real, grad_imag], axis=1)

            def add_patch(slot_index, grid):
                piece = lax.dynamic_index_in_dim(pieces, slot_index, 0, keepdims=False)
                row_at = centre[0][slot_index]
                col_at = centre[1][slot_index]
                current = lax.dynamic_slice(grid, (zero_index, row_at, col_at), (2, PS, PS))
                return lax.dynamic_update_slice(grid, current + piece, (zero_index, row_at, col_at))

            grad_padded = lax.fori_loop(0, SLOTS, add_patch, grad_padded)
            return (grad_padded, grad_probe + probe_part), None

        start = (jnp.zeros(padded.shape, jnp.float32), jnp.zeros(probe_field.shape, jnp.float32))
        (grad_padded, grad_probe), unused = lax.scan(per_tile, start, (centres, measured, totals))
        object_field = object_field - step_object * grad_padded[:, HALF:HALF + NR, HALF:HALF + NC]
        probe_field = probe_field - (step_probe / TOTAL_POS) * grad_probe
    return object_field, probe_field
```

```python
import math

import jax
import jax.numpy as jnp
from jax import lax
from jax.experimental import pallas as pl
from jax.experimental.pallas import tpu as pltpu
from jax.sharding import PartitionSpec as P

ITERS = 2


step_object = 0.25
step_probe = 0.5
floor_amp = 0.5
LANES = 128


def padded(cells, sides, width):
    for axis, dim in sides:
        count = lax.axis_size(axis)
        ends = count - 1
        head = lax.slice_in_dim(cells, 0, width, axis=dim)
        tail = lax.slice_in_dim(cells, cells.shape[dim] - width, cells.shape[dim], axis=dim)
        cells = jnp.concatenate(
            [
                lax.ppermute(tail, axis, [(i, (i + 1) % count) for i in range(ends)]),
                cells,
                lax.ppermute(head, axis, [((i + 1) % count, i) for i in range(ends)]),
            ],
            axis=dim,
        )
    return cells


def from_behind(value, axis, steps):
    count = lax.axis_size(axis)
    initial, last = (max(0, -steps), min(count, count - steps))
    return lax.ppermute(value, axis, [(source, source + steps) for source in range(initial, last)])


def tables(size):
    index = jnp.arange(size, dtype=jnp.int32)
    wrapped = index[:, None] * index[None, :] % size
    angle = 2.0 * math.pi / size * wrapped.astype(jnp.float32)
    scaling = 1.0 / math.sqrt(size)
    cosine, sine = (jnp.cos(angle) * scaling, jnp.sin(angle) * scaling)
    both = jnp.stack(
        [
            jnp.block([[cosine, -sine], [sine, cosine]]),
            jnp.block([[cosine, sine], [-sine, cosine]]),
        ]
    )
    high = lax.reduce_precision(both, 8, 7)
    return (high.astype(jnp.bfloat16), (both - high).astype(jnp.bfloat16))


def extend_object(object_field, rim_width):
    return padded(object_field, (("row", 1), ("col", 2)), rim_width)


def fold_edges(grid, tile_rows, tile_cols, rim_width):
    from_left = from_behind(grid[:, :, tile_cols + rim_width :], "col", 1)
    from_right = from_behind(grid[:, :, :rim_width], "col", -1)
    middle = grid[:, :, rim_width : tile_cols + rim_width]
    middle = middle.at[:, :, :rim_width].add(from_left)
    middle = middle.at[:, :, tile_cols - rim_width :].add(from_right)
    from_above = from_behind(middle[:, tile_rows + rim_width :, :], "row", 1)
    from_below = from_behind(middle[:, :rim_width, :], "row", -1)
    inner = middle[:, rim_width : tile_rows + rim_width, :]
    inner = inner.at[:, :rim_width, :].add(from_above)
    inner = inner.at[:, tile_rows - rim_width :, :].add(from_below)
    return inner


def update_probe(probe_field, grad_probe, scaling):
    total = lax.psum(grad_probe, ("row", "col"))
    return probe_field - scaling * total


def split(value):
    high = value.astype(jnp.bfloat16)
    return high, (value - high.astype(jnp.float32)).astype(jnp.bfloat16)


def dot(a, b):
    return jnp.dot(a, b, preferred_element_type=jnp.float32)


def times_right(value, table_high, table_low):
    high, low = split(value)
    return dot(high, table_high) + dot(low, table_high) + dot(high, table_low)


def times_left(table_high, table_low, value):
    high, low = split(value)
    return dot(table_high, high) + dot(table_low, high) + dot(table_high, low)


def swap_blocks(value):
    n = LANES
    return jnp.concatenate(
        [
            jnp.concatenate([value[:n, :n], value[n:, :n]], axis=1),
            jnp.concatenate([value[:n, n:], value[n:, n:]], axis=1),
        ],
        axis=0,
    )


def take_patch(source, part, place):
    n = LANES
    high_row, low_row, base, shift = place
    rows = n + 8
    lane = lax.broadcasted_iota(jnp.int32, (rows, n), 1)
    left = source[part, pl.ds(high_row, rows), pl.ds(base, n)]
    right = source[part, pl.ds(high_row, rows), pl.ds(base + n, n)]
    both = pltpu.roll(jnp.where(lane >= shift, left, right), (n - shift) % n, 1)
    turned = pltpu.roll(both.reshape(rows // 8, 8, n), (8 - low_row) % 8, 1)
    line = lax.broadcasted_iota(jnp.int32, (n // 8, 8, n), 1)
    return jnp.where(line < 8 - low_row, turned[:-1], turned[1:]).reshape(n, n)


def add_piece(grid, part, place, piece):
    n = LANES
    high_row, low_row, base, shift = place
    rows = n + 8
    turned = pltpu.roll(pltpu.roll(piece, shift, 1).reshape(n // 8, 8, n), low_row, 1)
    none = jnp.zeros((1, 8, n), jnp.float32)
    line = lax.broadcasted_iota(jnp.int32, (rows // 8, 8, n), 1)
    tall = jnp.where(
        line >= low_row,
        jnp.concatenate([turned, none], axis=0),
        jnp.concatenate([none, turned], axis=0),
    ).reshape(rows, n)
    lane = lax.broadcasted_iota(jnp.int32, (rows, n), 1)
    at_rows = pl.ds(high_row, rows)
    grid[part, at_rows, pl.ds(base, n)] += jnp.where(lane >= shift, tall, 0.0)
    grid[part, at_rows, pl.ds(base + n, n)] += jnp.where(lane >= shift, 0.0, tall)


def slots_kernel(
    rows, cols, count, extended, probe, amplitude, high_tables, low_tables, grid, grad_probe
):
    n = LANES
    slot_count = amplitude.shape[0]
    grid[...] = jnp.zeros_like(grid)
    probe_real = probe[0]
    probe_imag = probe[1]
    probe_sum_real = jnp.zeros((n, n), jnp.float32)
    probe_sum_imag = jnp.zeros((n, n), jnp.float32)
    a_high, b_high = high_tables[0], high_tables[1]
    a_low, b_low = low_tables[0], low_tables[1]
    for pair in range(slot_count // 2):
        patches = []
        exits = []
        places = []
        for slot in (2 * pair, 2 * pair + 1):
            row_at = rows[slot]
            col_at = cols[slot]
            place = (
                pl.multiple_of(row_at // 8 * 8, 8),
                row_at % 8,
                pl.multiple_of(col_at // n * n, n),
                col_at % n,
            )
            patch = [take_patch(extended, part, place) for part in range(2)]
            patches.append(patch)
            places.append(place)
            exits.append(
                jnp.concatenate(
                    [
                        probe_real * patch[0] - probe_imag * patch[1],
                        probe_real * patch[1] + probe_imag * patch[0],
                    ],
                    axis=1,
                )
            )
        wave = times_right(jnp.concatenate(exits, axis=0), a_high, a_low)
        far = times_left(b_high, b_low, swap_blocks(wave))
        far_real, far_imag = far[:n], far[n:]
        measured = jnp.concatenate([amplitude[2 * pair], amplitude[2 * pair + 1]], axis=1)
        power = far_real * far_real + far_imag * far_imag
        keeping = 1.0 - measured * lax.rsqrt(jnp.maximum(power, floor_amp * floor_amp))
        kept = jnp.concatenate([far_real * keeping, far_imag * keeping], axis=0)
        back = times_left(a_high, a_low, kept)
        change = times_right(swap_blocks(back), b_high, b_low)
        for k in range(2):
            usable = jnp.where(2 * pair + k < count[0], 1.0, 0.0)
            change_real = change[k * n : (k + 1) * n, :n] * usable
            change_imag = change[k * n : (k + 1) * n, n:] * usable
            object_real, object_imag = patches[k]
            probe_sum_real += object_real * change_real + object_imag * change_imag
            probe_sum_imag += object_real * change_imag - object_imag * change_real
            pieces = (
                probe_real * change_real + probe_imag * change_imag,
                probe_real * change_imag - probe_imag * change_real,
            )
            for part in range(2):
                add_piece(grid, part, places[k], pieces[part])
    grad_probe[0] = probe_sum_real
    grad_probe[1] = probe_sum_imag


def gradients(rows, cols, count, extended, probe, amplitude, high_tables, low_tables):
    smem = pl.BlockSpec(memory_space=pltpu.SMEM)
    vmem = pl.BlockSpec(memory_space=pltpu.VMEM)
    return pl.pallas_call(
        slots_kernel,
        out_shape=(
            jax.ShapeDtypeStruct(extended.shape, jnp.float32),
            jax.ShapeDtypeStruct(probe.shape, jnp.float32),
        ),
        in_specs=[smem] * 3 + [vmem] * 5,
        out_specs=(vmem, vmem),
        compiler_params=pltpu.CompilerParams(vmem_limit_bytes=40 * 1024 * 1024),
    )(rows, cols, count, extended, probe, amplitude, high_tables, low_tables)


def shards(object_field, probe_field, amplitudes, positions, counts):
    tile_rows = object_field.shape[1]
    tile_cols = object_field.shape[2]
    patch_size = probe_field.shape[-1]
    rim_width = patch_size // 2
    slot_count = amplitudes.shape[2]
    recorded = lax.axis_size("row") * lax.axis_size("col") * (2 * slot_count // 3)
    scaling = step_probe / recorded
    high_tables, low_tables = tables(patch_size)
    start_rows = positions[0, 0, 0] - lax.axis_index("row") * tile_rows
    start_cols = positions[0, 0, 1] - lax.axis_index("col") * tile_cols
    measured = amplitudes[0, 0]
    for iteration in range(ITERS):
        extended = extend_object(object_field, rim_width)
        grid, grad_probe = gradients(
            start_rows, start_cols, counts[0], extended, probe_field, measured,
            high_tables, low_tables,
        )
        grad_object = fold_edges(grid, tile_rows, tile_cols, rim_width)
        object_field = object_field - step_object * grad_object
        probe_field = update_probe(probe_field, grad_probe, scaling)
    return (object_field, probe_field)


def solution(mesh):
    return jax.shard_map(
        shards,
        mesh=mesh,
        in_specs=(
            P(None, ("parts", "row"), "col"),
            P(),
            P("row", "col", "parts", None, None),
            P("row", "col", "parts", None),
            P(("parts", "row"), "col"),
        ),
        out_specs=(P(None, ("parts", "row"), "col"), P("parts", None, None)),
        check_vma=False,
    )
```

```python
import functools
import math

import jax
import jax.numpy as jnp
from jax import lax
from jax.experimental import pallas as pl
from jax.experimental.pallas import tpu as pltpu
from jax.sharding import PartitionSpec as P

ITERS = 2


step_object = 0.25
step_probe = 0.5
floor_amp = 0.5
LANES = 128


def tables(size):
    index = jnp.arange(size, dtype=jnp.int32)
    wrapped = index[:, None] * index[None, :] % size
    angle = 2.0 * math.pi / size * wrapped.astype(jnp.float32)
    scaling = 1.0 / math.sqrt(size)
    cosine, sine = (jnp.cos(angle) * scaling, jnp.sin(angle) * scaling)
    both = jnp.stack(
        [
            jnp.block([[cosine, -sine], [sine, cosine]]),
            jnp.block([[cosine, sine], [-sine, cosine]]),
        ]
    )
    high = lax.reduce_precision(both, 8, 7)
    return (high.astype(jnp.bfloat16), (both - high).astype(jnp.bfloat16))


def split(value):
    high = value.astype(jnp.bfloat16)
    return high, (value - high.astype(jnp.float32)).astype(jnp.bfloat16)


def dot(a, b):
    return jnp.dot(a, b, preferred_element_type=jnp.float32)


def times_right(value, table_high, table_low):
    high, low = split(value)
    return dot(high, table_high) + dot(low, table_high) + dot(high, table_low)


def times_left(table_high, table_low, value):
    high, low = split(value)
    return dot(table_high, high) + dot(table_low, high) + dot(table_high, low)


def swap_blocks(value):
    n = LANES
    return jnp.concatenate(
        [
            jnp.concatenate([value[:n, :n], value[n:, :n]], axis=1),
            jnp.concatenate([value[:n, n:], value[n:, n:]], axis=1),
        ],
        axis=0,
    )


def take_patch(source, part, place):
    n = LANES
    high_row, low_row, base, shift = place
    rows = n + 8
    lane = lax.broadcasted_iota(jnp.int32, (rows, n), 1)
    left = source[part, pl.ds(high_row, rows), pl.ds(base, n)]
    right = source[part, pl.ds(high_row, rows), pl.ds(base + n, n)]
    both = pltpu.roll(jnp.where(lane >= shift, left, right), (n - shift) % n, 1)
    turned = pltpu.roll(both.reshape(rows // 8, 8, n), (8 - low_row) % 8, 1)
    line = lax.broadcasted_iota(jnp.int32, (n // 8, 8, n), 1)
    return jnp.where(line < 8 - low_row, turned[:-1], turned[1:]).reshape(n, n)


def add_piece(grid, part, place, piece):
    n = LANES
    high_row, low_row, base, shift = place
    rows = n + 8
    turned = pltpu.roll(pltpu.roll(piece, shift, 1).reshape(n // 8, 8, n), low_row, 1)
    none = jnp.zeros((1, 8, n), jnp.float32)
    line = lax.broadcasted_iota(jnp.int32, (rows // 8, 8, n), 1)
    tall = jnp.where(
        line >= low_row,
        jnp.concatenate([turned, none], axis=0),
        jnp.concatenate([none, turned], axis=0),
    ).reshape(rows, n)
    lane = lax.broadcasted_iota(jnp.int32, (rows, n), 1)
    at_rows = pl.ds(high_row, rows)
    grid[part, at_rows, pl.ds(base, n)] += jnp.where(lane >= shift, tall, 0.0)
    grid[part, at_rows, pl.ds(base + n, n)] += jnp.where(lane >= shift, 0.0, tall)


def slots_kernel(
    rows, cols, count, extended, probe, amplitude, high_tables, low_tables, grid, grad_probe
):
    n = LANES
    slot_count = amplitude.shape[0]
    grid[...] = jnp.zeros_like(grid)
    probe_real = probe[0]
    probe_imag = probe[1]
    probe_sum_real = jnp.zeros((n, n), jnp.float32)
    probe_sum_imag = jnp.zeros((n, n), jnp.float32)
    a_high, b_high = high_tables[0], high_tables[1]
    a_low, b_low = low_tables[0], low_tables[1]
    for pair in range(slot_count // 2):
        patches = []
        exits = []
        places = []
        for slot in (2 * pair, 2 * pair + 1):
            row_at = rows[slot]
            col_at = cols[slot]
            place = (
                pl.multiple_of(row_at // 8 * 8, 8),
                row_at % 8,
                pl.multiple_of(col_at // n * n, n),
                col_at % n,
            )
            patch = [take_patch(extended, part, place) for part in range(2)]
            patches.append(patch)
            places.append(place)
            exits.append(
                jnp.concatenate(
                    [
                        probe_real * patch[0] - probe_imag * patch[1],
                        probe_real * patch[1] + probe_imag * patch[0],
                    ],
                    axis=1,
                )
            )
        wave = times_right(jnp.concatenate(exits, axis=0), a_high, a_low)
        far = times_left(b_high, b_low, swap_blocks(wave))
        far_real, far_imag = far[:n], far[n:]
        measured = jnp.concatenate([amplitude[2 * pair], amplitude[2 * pair + 1]], axis=1)
        power = far_real * far_real + far_imag * far_imag
        keeping = 1.0 - measured * lax.rsqrt(jnp.maximum(power, floor_amp * floor_amp))
        kept = jnp.concatenate([far_real * keeping, far_imag * keeping], axis=0)
        back = times_left(a_high, a_low, kept)
        change = times_right(swap_blocks(back), b_high, b_low)
        for k in range(2):
            usable = jnp.where(2 * pair + k < count[0], 1.0, 0.0)
            change_real = change[k * n : (k + 1) * n, :n] * usable
            change_imag = change[k * n : (k + 1) * n, n:] * usable
            object_real, object_imag = patches[k]
            probe_sum_real += object_real * change_real + object_imag * change_imag
            probe_sum_imag += object_real * change_imag - object_imag * change_real
            pieces = (
                probe_real * change_real + probe_imag * change_imag,
                probe_real * change_imag - probe_imag * change_real,
            )
            for part in range(2):
                add_piece(grid, part, places[k], pieces[part])
    grad_probe[0] = probe_sum_real
    grad_probe[1] = probe_sum_imag


def gradients(rows, cols, count, extended, probe, amplitude, high_tables, low_tables):
    smem = pl.BlockSpec(memory_space=pltpu.SMEM)
    vmem = pl.BlockSpec(memory_space=pltpu.VMEM)
    return pl.pallas_call(
        slots_kernel,
        out_shape=(
            jax.ShapeDtypeStruct(extended.shape, jnp.float32),
            jax.ShapeDtypeStruct(probe.shape, jnp.float32),
        ),
        in_specs=[smem] * 3 + [vmem] * 5,
        out_specs=(vmem, vmem),
        compiler_params=pltpu.CompilerParams(vmem_limit_bytes=40 * 1024 * 1024),
    )(rows, cols, count, extended, probe, amplitude, high_tables, low_tables)


MESH = pl.DeviceIdType.MESH


class Links:
    def __init__(self, sizes, send_sem, recv_sem):
        self.sizes = sizes
        self.send_sem = send_sem
        self.recv_sem = recv_sem
        self.at = {axis: lax.axis_index(axis) for axis in sizes}
        self.used = 0

    def has(self, axis, step):
        return self.at[axis] > 0 if step < 0 else self.at[axis] < self.sizes[axis] - 1

    def peer(self, axis, step):
        size = self.sizes[axis]
        return lax.rem(self.at[axis] + (step + size), size)

    def greet(self, everyone):
        barrier = pltpu.get_barrier_semaphore()
        if everyone:
            for axis, size in self.sizes.items():
                for step in range(1, size):
                    pl.semaphore_signal(
                        barrier, inc=1, device_id={axis: self.peer(axis, step)}, device_id_type=MESH
                    )
            pl.semaphore_wait(barrier, sum(size - 1 for size in self.sizes.values()))
            return
        for axis in self.sizes:
            for step in (-1, 1):
                @pl.when(self.has(axis, step))
                def signal():
                    pl.semaphore_signal(
                        barrier, inc=1, device_id={axis: self.peer(axis, step)}, device_id_type=MESH
                    )
        peers = 0
        for axis in self.sizes:
            for step in (-1, 1):
                peers = peers + jnp.where(self.has(axis, step), 1, 0)
        pl.semaphore_wait(barrier, peers)

    def copy(self, src, dst, axis, step):
        number = self.used
        self.used += 1
        return pltpu.make_async_remote_copy(
            src_ref=src,
            dst_ref=dst,
            send_sem=self.send_sem.at[number],
            recv_sem=self.recv_sem.at[number],
            device_id={axis: self.peer(axis, step)},
            device_id_type=MESH,
        )

    def edge(self, src, dst, axis, step):
        return Edge(self, self.copy(src, dst, axis, step), axis, step)


class Edge:
    def __init__(self, links, copy, axis, step):
        self.links, self.copy, self.axis, self.step = links, copy, axis, step

    def start(self):
        pl.when(self.links.has(self.axis, self.step))(lambda: self.copy.start())

    def wait_send(self):
        pl.when(self.links.has(self.axis, self.step))(lambda: self.copy.wait_send())

    def wait_recv(self):
        pl.when(self.links.has(self.axis, -self.step))(lambda: self.copy.wait_recv())


def clear(links, axis, step, ref):
    @pl.when(jnp.logical_not(links.has(axis, step)))
    def fill():
        ref[...] = jnp.zeros(ref.shape, ref.dtype)


STEPS = (-1, 1)


def halo_kernel(sizes, tile, ext, band_out, band_in, corner_out, corner_in, send_sem, recv_sem):
    n = LANES
    half = n // 2
    tile_rows, tile_cols = tile.shape[1:]
    last = tile_cols + n
    links = Links(sizes, send_sem, recv_sem)
    links.greet(False)
    rows = []
    for step in STEPS:
        src = tile.at[:, pl.ds(0 if step < 0 else tile_rows - half, half), :]
        to = tile_rows + half if step < 0 else 0
        rows.append(
            links.edge(src, ext.at[:, pl.ds(to, half), pl.ds(n, tile_cols)], "row", step)
        )
    lane = lax.broadcasted_iota(jnp.int32, (tile_rows, n), 1)
    bands = []
    for k, step in enumerate(STEPS):
        at = 0 if step < 0 else tile_cols - n
        real = tile[0, :, at : at + n]
        imag = pltpu.roll(tile[1, :, at : at + n], half, 1)
        low, high = (real, imag) if step < 0 else (imag, real)
        band_out[k] = jnp.where(lane < half, low, high)
        clear(links, "col", -step, band_in.at[k])
        band = links.edge(band_out.at[k], band_in.at[k], "col", step)
        band.start()
        bands.append(band)
    for row in rows:
        row.start()
    for k, step in enumerate(STEPS):
        clear(links, "row", -step, corner_in.at[k])
        to = tile_rows + half if step < 0 else 0
        clear(links, "row", -step, ext.at[:, pl.ds(to, half), pl.ds(n, tile_cols)])
    ext[:, half : half + tile_rows, n : n + tile_cols] = tile[...]
    for k, step in enumerate(STEPS):
        bands[k].wait_recv()
        got = band_in[k]
        back = pltpu.roll(got, half, 1)
        at = last if step < 0 else 0
        keep = lane < half if step < 0 else lane >= half
        ext[0, half : half + tile_rows, at : at + n] = jnp.where(keep, got, 0.0)
        ext[1, half : half + tile_rows, at : at + n] = jnp.where(keep, back, 0.0)
    corners = []
    narrow = lax.broadcasted_iota(jnp.int32, (half, n), 1)
    for k, step in enumerate(STEPS):
        at = half if step < 0 else tile_rows
        for part in range(2):
            corner_out[k, part] = jnp.where(
                narrow >= half,
                ext[part, at : at + half, :n],
                ext[part, at : at + half, last : last + n],
            )
        corner = links.edge(corner_out.at[k], corner_in.at[k], "row", step)
        corner.start()
        corners.append(corner)
    for k, step in enumerate(STEPS):
        corners[k].wait_recv()
        to = tile_rows + half if step < 0 else 0
        for part in range(2):
            got = corner_in[k, part]
            ext[part, to : to + half, :n] = jnp.where(narrow >= half, got, 0.0)
            ext[part, to : to + half, last : last + n] = jnp.where(narrow < half, got, 0.0)
        rows[k].wait_recv()
    for edge in bands + rows + corners:
        edge.wait_send()


class ProbeSum:
    def __init__(self, links, scaling, probe, gradient, new_probe, shares, sums, total):
        self.links, self.scaling = links, scaling
        self.probe, self.new_probe = probe, new_probe
        self.shares, self.sums, self.total = shares, sums, total
        self.count = gradient.shape[0] // links.sizes["row"]
        self.mine = self.share(links.at["row"])
        self.gradient = gradient
        self.copies = []
        self.first = []
        for step in range(1, links.sizes["row"]):
            src = gradient.at[self.share(links.peer("row", step)), :]
            self.first.append(links.copy(src, shares.at[step - 1], "row", step))
        for copy in self.first:
            copy.start()

    def share(self, owner):
        return pl.ds(pl.multiple_of(owner * self.count, self.count), self.count)

    def across(self):
        links = self.links
        value = self.gradient[self.mine, :]
        for k, copy in enumerate(self.first):
            copy.wait_recv()
            value = value + self.shares[k]
        own = links.at["col"]
        self.sums[own] = value
        self.second = []
        for step in range(1, links.sizes["col"]):
            self.second.append(links.copy(self.sums.at[own], self.sums.at[own], "col", step))
        for copy in self.second:
            copy.start()

    def spread(self):
        links = self.links
        for copy in self.second:
            copy.wait_recv()
        value = self.sums[0]
        for k in range(1, links.sizes["col"]):
            value = value + self.sums[k]
        self.new_probe[self.mine, :] = self.probe[self.mine, :] - self.scaling * value
        self.third = []
        for step in range(1, links.sizes["row"]):
            ref = self.new_probe.at[self.mine, :]
            self.third.append(links.copy(ref, ref, "row", step))
        for copy in self.third:
            copy.start()

    def finish(self):
        for copy in self.third:
            copy.wait_recv()
        for copy in self.first + self.second + self.third:
            copy.wait_send()


def middle_kernel(
    sizes, scaling, ext, grid, probe, gradient, new_ext, new_probe,
    edge_out, edge_in, inner_out, inner_in, side_out, side_in,
    shares, sums, total, send_sem, recv_sem,
):
    n = LANES
    half = n // 2
    high = ext.shape[1]
    last = ext.shape[2] - n
    links = Links(sizes, send_sem, recv_sem)
    links.greet(True)
    summed = ProbeSum(links, scaling, probe, gradient, new_probe, shares, sums, total)
    upper = lax.broadcasted_iota(jnp.int32, (n, n), 1) >= half

    def block(part, at, k):
        return grid[part, at : at + n, k : k + n]

    def band(part, at, side):
        base = 0 if side == 0 else last - n
        return jnp.where(upper, block(part, at, base), block(part, at, base + n))

    tops = (0, high - n)
    edges = []
    for k, step in enumerate(STEPS):
        for part in range(2):
            for side in range(2):
                edge_out[k, part, side] = band(part, tops[k], side)
        clear(links, "row", -step, edge_in.at[k])
        edge = links.edge(edge_out.at[k], edge_in.at[k], "row", step)
        edge.start()
        edges.append(edge)
    sides = []
    for k, step in enumerate(STEPS):
        for part in range(2):
            side_out[k, 1, part] = band(part, n, k)
        clear(links, "col", -step, side_in.at[k])
        side = links.edge(side_out.at[k, 1], side_in.at[k, 1], "col", step)
        side.start()
        sides.append(side)
    inners = []
    for k, step in enumerate(STEPS):
        for part in range(2):
            inner_out[k, part, :, :n] = jnp.where(
                upper, block(part, tops[k], n), block(part, tops[k], last - n)
            )
            inner_out[k, part, :, n:] = grid[part, tops[k] : tops[k] + n, 2 * n : last - n]
        clear(links, "row", -step, inner_in.at[k])
        inner = links.edge(inner_out.at[k], inner_in.at[k], "row", step)
        inner.start()
        inners.append(inner)
    summed.across()
    for k, step in enumerate(STEPS):
        edges[1 - k].wait_recv()
        for side, way in enumerate(STEPS):
            for part in range(2):
                side_out[side, 2 * k, part] = edge_out[k, part, side] + edge_in[1 - k, part, side]
            corner = links.edge(side_out.at[side, 2 * k], side_in.at[side, 2 * k], "col", way)
            corner.start()
            sides.append(corner)
    summed.spread()
    for edge in inners + sides:
        edge.wait_recv()
    for k in range(3):
        at = k * n
        for part in range(2):
            ends = [side_out[side, k, part] + side_in[1 - side, k, part] for side in range(2)]
            if k == 1:
                mixed = jnp.where(upper, block(part, at, n), block(part, at, last - n))
                flat = grid[part, at : at + n, 2 * n : last - n]
            else:
                mixed = inner_out[k // 2, part, :, :n] + inner_in[1 - k // 2, part, :, :n]
                flat = inner_out[k // 2, part, :, n:] + inner_in[1 - k // 2, part, :, n:]

            def put(lo, hi, value):
                new_ext[part, at : at + n, lo:hi] = (
                    ext[part, at : at + n, lo:hi] - step_object * value
                )

            put(0, n, jnp.where(upper, ends[0], 0.0))
            put(n, 2 * n, jnp.where(upper, mixed, ends[0]))
            put(2 * n, last - n, flat)
            put(last - n, last, jnp.where(upper, ends[1], mixed))
            put(last, last + n, jnp.where(upper, 0.0, ends[1]))
    clear(links, "row", -1, new_ext.at[:, pl.ds(0, half), :])
    clear(links, "row", 1, new_ext.at[:, pl.ds(high - half, half), :])
    clear(links, "col", -1, new_ext.at[:, :, pl.ds(0, n)])
    clear(links, "col", 1, new_ext.at[:, :, pl.ds(last, n)])
    for edge in edges + inners + sides:
        edge.wait_send()
    summed.finish()


def final_kernel(
    sizes, scaling, ext, grid, probe, gradient, tile, new_probe,
    rim_out, rim_in, flat_in, mid_out, mid_in, end_out, end_in,
    shares, sums, total, send_sem, recv_sem,
):
    n = LANES
    half = n // 2
    high = ext.shape[1]
    last = ext.shape[2] - n
    tile_rows, tile_cols = tile.shape[1:]
    links = Links(sizes, send_sem, recv_sem)
    links.greet(True)
    summed = ProbeSum(links, scaling, probe, gradient, new_probe, shares, sums, total)
    upper = lax.broadcasted_iota(jnp.int32, (half, n), 1) >= half
    tall = lax.broadcasted_iota(jnp.int32, (n, n), 1) >= half
    outer = (0, high - half)
    inner = (half, high - n)
    rims = []
    flats = []
    for k, step in enumerate(STEPS):
        at = outer[k]
        for part in range(2):
            rim_out[k, part] = jnp.where(
                upper, grid[part, at : at + half, :n], grid[part, at : at + half, last:]
            )
        clear(links, "row", -step, rim_in.at[k])
        rim = links.edge(rim_out.at[k], rim_in.at[k], "row", step)
        rim.start()
        rims.append(rim)
        clear(links, "row", -step, flat_in.at[k])
        flats.append(
            links.edge(
                grid.at[:, pl.ds(at, half), pl.ds(n, tile_cols)], flat_in.at[k], "row", step
            )
        )

    def fuse(mask, side, real, imag):
        turned = pltpu.roll(imag, half, 1)
        return jnp.where(mask, real, turned) if side == 0 else jnp.where(mask, turned, real)

    middles = []
    for side, way in enumerate(STEPS):
        at = 0 if side == 0 else last
        mid_out[side] = fuse(
            tall, side, grid[0, n : high - n, at : at + n], grid[1, n : high - n, at : at + n]
        )
        clear(links, "col", -way, mid_in.at[side])
        clear(links, "col", -way, end_in.at[side])
        middle = links.edge(mid_out.at[side], mid_in.at[side], "col", way)
        middle.start()
        middles.append(middle)
    for flat in flats:
        flat.start()
    summed.across()
    for k in range(2):
        rims[1 - k].wait_recv()
        at = inner[k]
        for side, way in enumerate(STEPS):
            base = 0 if side == 0 else last
            values = [
                grid[part, at : at + half, base : base + n] + rim_in[1 - k, part]
                for part in range(2)
            ]
            end_out[side, k] = fuse(upper, side, values[0], values[1])
            end = links.edge(end_out.at[side, k], end_in.at[side, k], "col", way)
            end.start()
            middles.append(end)
    tile[:, half : tile_rows - half, :] = (
        ext[:, n : high - n, n:last] - step_object * grid[:, n : high - n, n:last]
    )
    summed.spread()
    for k in range(2):
        flats[1 - k].wait_recv()
        at = inner[k]
        tile[:, at - half : at, :] = ext[:, at : at + half, n:last] - step_object * (
            grid[:, at : at + half, n:last] + flat_in[1 - k]
        )
    for middle in middles:
        middle.wait_recv()

    def land(at, count, side, value, mask):
        base = tile_cols - n if side == 0 else 0
        keep = mask if side == 0 else jnp.logical_not(mask)
        turned = pltpu.roll(value, half, 1)
        for part, piece in enumerate((value, turned)):
            tile[part, at : at + count, base : base + n] -= step_object * jnp.where(
                keep, piece, 0.0
            )

    for side in range(2):
        land(half, n, side, mid_in[side], tall)
        for k in range(2):
            land(inner[k] - half, half, side, end_in[side, k], upper)
    for edge in rims + flats + middles:
        edge.wait_send()
    summed.finish()


def remote(kernel, collective_id, sizes, outs, scratch, copies, *operands):
    vmem = pl.BlockSpec(memory_space=pltpu.VMEM)
    return pl.pallas_call(
        kernel,
        out_shape=[jax.ShapeDtypeStruct(shape, jnp.float32) for shape in outs],
        in_specs=[vmem] * len(operands),
        out_specs=[vmem] * len(outs),
        scratch_shapes=[pltpu.VMEM(shape, jnp.float32) for shape in scratch]
        + [pltpu.SemaphoreType.DMA((copies,))] * 2,
        compiler_params=pltpu.CompilerParams(
            collective_id=collective_id,
            has_side_effects=True,
            vmem_limit_bytes=40 * 1024 * 1024,
        ),
    )(*operands)


def shards(object_field, probe_field, amplitudes, positions, counts):
    tile_rows = object_field.shape[1]
    tile_cols = object_field.shape[2]
    n = probe_field.shape[-1]
    half = n // 2
    slot_count = amplitudes.shape[2]
    sizes = {axis: lax.axis_size(axis) for axis in ("row", "col")}
    recorded = sizes["row"] * sizes["col"] * (2 * slot_count // 3)
    scaling = step_probe / recorded
    high_tables, low_tables = tables(n)
    start_rows = positions[0, 0, 0] - lax.axis_index("row") * tile_rows
    start_cols = positions[0, 0, 1] - lax.axis_index("col") * tile_cols + half
    measured = amplitudes[0, 0]
    wide = (2, tile_rows + n, tile_cols + 2 * n)
    share = 2 * n // sizes["row"]
    probe_scratch = [
        (sizes["row"] - 1, share, n), (sizes["col"], share, n), (8, n),
    ]
    probe_copies = 2 * (sizes["row"] - 1) + sizes["col"] - 1
    (extended,) = remote(
        functools.partial(halo_kernel, sizes), 0, sizes, [wide],
        [(2, tile_rows, n)] * 2 + [(2, 2, half, n)] * 2, 6, object_field,
    )
    for iteration in range(ITERS):
        grid, grad_probe = gradients(
            start_rows, start_cols, counts[0], extended, probe_field, measured,
            high_tables, low_tables,
        )
        operands = (
            extended, grid, probe_field.reshape(2 * n, n), grad_probe.reshape(2 * n, n)
        )
        if iteration < ITERS - 1:
            extended, probe_field = remote(
                functools.partial(middle_kernel, sizes, scaling), 1, sizes, [wide, (2 * n, n)],
                [(2, 2, 2, n, n)] * 2 + [(2, 2, n, tile_cols - n)] * 2 + [(2, 3, 2, n, n)] * 2
                + probe_scratch, 10 + probe_copies, *operands,
            )
        else:
            object_field, probe_field = remote(
                functools.partial(final_kernel, sizes, scaling), 2, sizes,
                [object_field.shape, (2 * n, n)],
                [(2, 2, half, n)] * 2 + [(2, 2, half, tile_cols)] + [(2, n, n)] * 2
                + [(2, 2, half, n)] * 2 + probe_scratch, 10 + probe_copies, *operands,
            )
        probe_field = probe_field.reshape(2, n, n)
    return (object_field, probe_field)


def solution(mesh):
    return jax.shard_map(
        shards,
        mesh=mesh,
        in_specs=(
            P(None, ("parts", "row"), "col"),
            P(),
            P("row", "col", "parts", None, None),
            P("row", "col", "parts", None),
            P(("parts", "row"), "col"),
        ),
        out_specs=(P(None, ("parts", "row"), "col"), P("parts", None, None)),
        check_vma=False,
    )
```

```python
import functools
import math

import jax
import jax.numpy as jnp
import numpy as np
from jax import lax
from jax.experimental import pallas as pl
from jax.experimental.pallas import tpu as pltpu
from jax.sharding import PartitionSpec as P

ITERS = 2


step_object = 0.25
step_probe = 0.5
floor_amp = 0.5
LANES = 128
GROUP = 4


def tables(size):
    index = np.arange(size)
    angle = 2.0 * math.pi / size * (index[:, None] * index[None, :] % size)
    scaling = 1.0 / math.sqrt(size)
    cosine, sine = (np.cos(angle) * scaling, np.sin(angle) * scaling)
    both = np.stack(
        [
            np.block([[cosine, -sine], [sine, cosine]]),
            np.block([[cosine, sine], [-sine, cosine]]),
        ]
    )
    high = both.astype(jnp.bfloat16)
    low = (both - high.astype(np.float64)).astype(jnp.bfloat16)
    return (jnp.asarray(high), jnp.asarray(low))


def split(value):
    high = value.astype(jnp.bfloat16)
    return high, (value - high.astype(jnp.float32)).astype(jnp.bfloat16)


def dot(a, b):
    return jnp.dot(a, b, preferred_element_type=jnp.float32)


def times_right(value, table_high, table_low):
    high, low = split(value)
    return dot(high, table_high) + dot(low, table_high) + dot(high, table_low)


def times_left(table_high, table_low, value):
    high, low = split(value)
    return dot(table_high, high) + dot(table_low, high) + dot(table_high, low)


def swap_blocks(value):
    n = LANES
    down, across = value.shape[0] // n, value.shape[1] // n
    return jnp.concatenate(
        [
            jnp.concatenate(
                [value[i * n : (i + 1) * n, j * n : (j + 1) * n] for i in range(down)], axis=1
            )
            for j in range(across)
        ],
        axis=0,
    )


def take_patch(source, part, place):
    n = LANES
    high_row, low_row, base, shift = place
    rows = n + 8
    lane = lax.broadcasted_iota(jnp.int32, (rows, n), 1)
    left = source[part, pl.ds(high_row, rows), pl.ds(base, n)]
    right = source[part, pl.ds(high_row, rows), pl.ds(base + n, n)]
    both = pltpu.roll(jnp.where(lane >= shift, left, right), (n - shift) % n, 1)
    turned = pltpu.roll(both.reshape(rows // 8, 8, n), (8 - low_row) % 8, 1)
    line = lax.broadcasted_iota(jnp.int32, (n // 8, 8, n), 1)
    return jnp.where(line < 8 - low_row, turned[:-1], turned[1:]).reshape(n, n)


def add_piece(grid, part, place, piece):
    n = LANES
    high_row, low_row, base, shift = place
    rows = n + 8
    turned = pltpu.roll(pltpu.roll(piece, shift, 1).reshape(n // 8, 8, n), low_row, 1)
    none = jnp.zeros((1, 8, n), jnp.float32)
    line = lax.broadcasted_iota(jnp.int32, (rows // 8, 8, n), 1)
    tall = jnp.where(
        line >= low_row,
        jnp.concatenate([turned, none], axis=0),
        jnp.concatenate([none, turned], axis=0),
    ).reshape(rows, n)
    lane = lax.broadcasted_iota(jnp.int32, (rows, n), 1)
    at_rows = pl.ds(high_row, rows)
    grid[part, at_rows, pl.ds(base, n)] += jnp.where(lane >= shift, tall, 0.0)
    grid[part, at_rows, pl.ds(base + n, n)] += jnp.where(lane >= shift, 0.0, tall)


def slots_kernel(
    centres, count, extended, probe, amplitude, high_tables, low_tables, grid, grad_probe
):
    n = LANES
    slot_count = amplitude.shape[0]
    grid[...] = jnp.zeros_like(grid)
    probe_real = probe[0]
    probe_imag = probe[1]
    probe_sum_real = jnp.zeros((n, n), jnp.float32)
    probe_sum_imag = jnp.zeros((n, n), jnp.float32)
    a_high, b_high = high_tables[0], high_tables[1]
    a_low, b_low = low_tables[0], low_tables[1]
    row_base = lax.axis_index("row") * (extended.shape[1] - n)
    col_base = lax.axis_index("col") * (extended.shape[2] - 2 * n) - n // 2
    for first in range(0, slot_count, GROUP):
        group = range(first, first + GROUP)
        patches = []
        exits = []
        places = []
        for slot in group:
            row_at = centres[0, slot] - row_base
            col_at = centres[1, slot] - col_base
            place = (
                pl.multiple_of(row_at // 8 * 8, 8),
                row_at % 8,
                pl.multiple_of(col_at // n * n, n),
                col_at % n,
            )
            patch = [take_patch(extended, part, place) for part in range(2)]
            patches.append(patch)
            places.append(place)
            exits.append(
                jnp.concatenate(
                    [
                        probe_real * patch[0] - probe_imag * patch[1],
                        probe_real * patch[1] + probe_imag * patch[0],
                    ],
                    axis=1,
                )
            )
        wave = times_right(jnp.concatenate(exits, axis=0), a_high, a_low)
        far = times_left(b_high, b_low, swap_blocks(wave))
        far_real, far_imag = far[:n], far[n:]
        measured = jnp.concatenate([amplitude[slot] for slot in group], axis=1)
        power = far_real * far_real + far_imag * far_imag
        keeping = 1.0 - measured * lax.rsqrt(jnp.maximum(power, floor_amp * floor_amp))
        kept = jnp.concatenate([far_real * keeping, far_imag * keeping], axis=0)
        back = times_left(a_high, a_low, kept)
        change = times_right(swap_blocks(back), b_high, b_low)
        for k, slot in enumerate(group):
            usable = jnp.where(slot < count[0, 0], 1.0, 0.0)
            change_real = change[k * n : (k + 1) * n, :n] * usable
            change_imag = change[k * n : (k + 1) * n, n:] * usable
            object_real, object_imag = patches[k]
            probe_sum_real += object_real * change_real + object_imag * change_imag
            probe_sum_imag += object_real * change_imag - object_imag * change_real
            pieces = (
                probe_real * change_real + probe_imag * change_imag,
                probe_real * change_imag - probe_imag * change_real,
            )
            for part in range(2):
                add_piece(grid, part, places[k], pieces[part])
    grad_probe[0] = probe_sum_real
    grad_probe[1] = probe_sum_imag


def gradients(centres, count, extended, probe, amplitude, high_tables, low_tables):
    smem = pl.BlockSpec(memory_space=pltpu.SMEM)
    vmem = pl.BlockSpec(memory_space=pltpu.VMEM)
    return pl.pallas_call(
        slots_kernel,
        out_shape=(
            jax.ShapeDtypeStruct(extended.shape, jnp.float32),
            jax.ShapeDtypeStruct(probe.shape, jnp.float32),
        ),
        in_specs=[smem] * 2 + [vmem] * 5,
        out_specs=(vmem, vmem),
        compiler_params=pltpu.CompilerParams(vmem_limit_bytes=40 * 1024 * 1024),
    )(centres, count, extended, probe, amplitude, high_tables, low_tables)


MESH = pl.DeviceIdType.MESH


class Links:
    def __init__(self, sizes, send_sem, recv_sem):
        self.sizes = sizes
        self.send_sem = send_sem
        self.recv_sem = recv_sem
        self.at = {axis: lax.axis_index(axis) for axis in sizes}
        self.used = 0

    def has(self, axis, step):
        return self.at[axis] > 0 if step < 0 else self.at[axis] < self.sizes[axis] - 1

    def peer(self, axis, step):
        size = self.sizes[axis]
        return lax.rem(self.at[axis] + (step + size), size)

    def greet(self, everyone):
        barrier = pltpu.get_barrier_semaphore()
        if everyone:
            for axis, size in self.sizes.items():
                for step in range(1, size):
                    pl.semaphore_signal(
                        barrier, inc=1, device_id={axis: self.peer(axis, step)}, device_id_type=MESH
                    )
            pl.semaphore_wait(barrier, sum(size - 1 for size in self.sizes.values()))
            return
        for axis in self.sizes:
            for step in (-1, 1):
                @pl.when(self.has(axis, step))
                def signal():
                    pl.semaphore_signal(
                        barrier, inc=1, device_id={axis: self.peer(axis, step)}, device_id_type=MESH
                    )
        peers = 0
        for axis in self.sizes:
            for step in (-1, 1):
                peers = peers + jnp.where(self.has(axis, step), 1, 0)
        pl.semaphore_wait(barrier, peers)

    def copy(self, src, dst, axis, step):
        number = self.used
        self.used += 1
        return pltpu.make_async_remote_copy(
            src_ref=src,
            dst_ref=dst,
            send_sem=self.send_sem.at[number],
            recv_sem=self.recv_sem.at[number],
            device_id={axis: self.peer(axis, step)},
            device_id_type=MESH,
        )

    def edge(self, src, dst, axis, step):
        return Edge(self, self.copy(src, dst, axis, step), axis, step)


class Edge:
    def __init__(self, links, copy, axis, step):
        self.links, self.copy, self.axis, self.step = links, copy, axis, step

    def start(self):
        pl.when(self.links.has(self.axis, self.step))(lambda: self.copy.start())

    def wait_send(self):
        pl.when(self.links.has(self.axis, self.step))(lambda: self.copy.wait_send())

    def wait_recv(self):
        pl.when(self.links.has(self.axis, -self.step))(lambda: self.copy.wait_recv())


def clear(links, axis, step, ref):
    @pl.when(jnp.logical_not(links.has(axis, step)))
    def fill():
        ref[...] = jnp.zeros(ref.shape, ref.dtype)


STEPS = (-1, 1)


def halo_kernel(sizes, tile, ext, band_out, band_in, corner_out, corner_in, send_sem, recv_sem):
    n = LANES
    half = n // 2
    tile_rows, tile_cols = tile.shape[1:]
    last = tile_cols + n
    links = Links(sizes, send_sem, recv_sem)
    links.greet(False)
    rows = []
    for step in STEPS:
        src = tile.at[:, pl.ds(0 if step < 0 else tile_rows - half, half), :]
        to = tile_rows + half if step < 0 else 0
        rows.append(
            links.edge(src, ext.at[:, pl.ds(to, half), pl.ds(n, tile_cols)], "row", step)
        )
    lane = lax.broadcasted_iota(jnp.int32, (tile_rows, n), 1)
    bands = []
    for k, step in enumerate(STEPS):
        at = 0 if step < 0 else tile_cols - n
        real = tile[0, :, at : at + n]
        imag = pltpu.roll(tile[1, :, at : at + n], half, 1)
        low, high = (real, imag) if step < 0 else (imag, real)
        band_out[k] = jnp.where(lane < half, low, high)
        clear(links, "col", -step, band_in.at[k])
        band = links.edge(band_out.at[k], band_in.at[k], "col", step)
        band.start()
        bands.append(band)
    for row in rows:
        row.start()
    for k, step in enumerate(STEPS):
        clear(links, "row", -step, corner_in.at[k])
        to = tile_rows + half if step < 0 else 0
        clear(links, "row", -step, ext.at[:, pl.ds(to, half), pl.ds(n, tile_cols)])
    ext[:, half : half + tile_rows, n : n + tile_cols] = tile[...]
    for k, step in enumerate(STEPS):
        bands[k].wait_recv()
        got = band_in[k]
        back = pltpu.roll(got, half, 1)
        at = last if step < 0 else 0
        keep = lane < half if step < 0 else lane >= half
        ext[0, half : half + tile_rows, at : at + n] = jnp.where(keep, got, 0.0)
        ext[1, half : half + tile_rows, at : at + n] = jnp.where(keep, back, 0.0)
    corners = []
    narrow = lax.broadcasted_iota(jnp.int32, (half, n), 1)
    for k, step in enumerate(STEPS):
        at = half if step < 0 else tile_rows
        for part in range(2):
            corner_out[k, part] = jnp.where(
                narrow >= half,
                ext[part, at : at + half, :n],
                ext[part, at : at + half, last : last + n],
            )
        corner = links.edge(corner_out.at[k], corner_in.at[k], "row", step)
        corner.start()
        corners.append(corner)
    for k, step in enumerate(STEPS):
        corners[k].wait_recv()
        to = tile_rows + half if step < 0 else 0
        for part in range(2):
            got = corner_in[k, part]
            ext[part, to : to + half, :n] = jnp.where(narrow >= half, got, 0.0)
            ext[part, to : to + half, last : last + n] = jnp.where(narrow < half, got, 0.0)
        rows[k].wait_recv()
    for edge in bands + rows + corners:
        edge.wait_send()


class ProbeSum:
    def __init__(self, links, scaling, probe, gradient, new_probe, shares, sums, total):
        self.links, self.scaling = links, scaling
        self.probe, self.new_probe = probe, new_probe
        self.shares, self.sums, self.total = shares, sums, total
        self.count = gradient.shape[0] // links.sizes["row"]
        self.mine = self.share(links.at["row"])
        self.gradient = gradient
        self.copies = []
        self.first = []
        for step in range(1, links.sizes["row"]):
            src = gradient.at[self.share(links.peer("row", step)), :]
            self.first.append(links.copy(src, shares.at[step - 1], "row", step))
        for copy in self.first:
            copy.start()

    def share(self, owner):
        return pl.ds(pl.multiple_of(owner * self.count, self.count), self.count)

    def across(self):
        links = self.links
        value = self.gradient[self.mine, :]
        for k, copy in enumerate(self.first):
            copy.wait_recv()
            value = value + self.shares[k]
        own = links.at["col"]
        self.sums[own] = value
        self.second = []
        for step in range(1, links.sizes["col"]):
            self.second.append(links.copy(self.sums.at[own], self.sums.at[own], "col", step))
        for copy in self.second:
            copy.start()

    def spread(self):
        links = self.links
        for copy in self.second:
            copy.wait_recv()
        value = self.sums[0]
        for k in range(1, links.sizes["col"]):
            value = value + self.sums[k]
        self.new_probe[self.mine, :] = self.probe[self.mine, :] - self.scaling * value
        self.third = []
        for step in range(1, links.sizes["row"]):
            ref = self.new_probe.at[self.mine, :]
            self.third.append(links.copy(ref, ref, "row", step))
        for copy in self.third:
            copy.start()

    def finish(self):
        for copy in self.third:
            copy.wait_recv()
        for copy in self.first + self.second + self.third:
            copy.wait_send()


def middle_kernel(
    sizes, scaling, ext, grid, probe, gradient, new_ext, new_probe,
    edge_out, edge_in, inner_out, inner_in, side_out, side_in,
    shares, sums, total, send_sem, recv_sem,
):
    n = LANES
    half = n // 2
    high = ext.shape[1]
    last = ext.shape[2] - n
    links = Links(sizes, send_sem, recv_sem)
    links.greet(True)
    summed = ProbeSum(links, scaling, probe, gradient, new_probe, shares, sums, total)
    upper = lax.broadcasted_iota(jnp.int32, (n, n), 1) >= half

    def block(part, at, k):
        return grid[part, at : at + n, k : k + n]

    def band(part, at, side):
        base = 0 if side == 0 else last - n
        return jnp.where(upper, block(part, at, base), block(part, at, base + n))

    tops = (0, high - n)
    edges = []
    for k, step in enumerate(STEPS):
        for part in range(2):
            for side in range(2):
                edge_out[k, part, side] = band(part, tops[k], side)
        clear(links, "row", -step, edge_in.at[k])
        edge = links.edge(edge_out.at[k], edge_in.at[k], "row", step)
        edge.start()
        edges.append(edge)
    sides = []
    for k, step in enumerate(STEPS):
        for part in range(2):
            side_out[k, 1, part] = band(part, n, k)
        clear(links, "col", -step, side_in.at[k])
        side = links.edge(side_out.at[k, 1], side_in.at[k, 1], "col", step)
        side.start()
        sides.append(side)
    inners = []
    for k, step in enumerate(STEPS):
        for part in range(2):
            inner_out[k, part, :, :n] = jnp.where(
                upper, block(part, tops[k], n), block(part, tops[k], last - n)
            )
            inner_out[k, part, :, n:] = grid[part, tops[k] : tops[k] + n, 2 * n : last - n]
        clear(links, "row", -step, inner_in.at[k])
        inner = links.edge(inner_out.at[k], inner_in.at[k], "row", step)
        inner.start()
        inners.append(inner)
    summed.across()
    for k, step in enumerate(STEPS):
        edges[1 - k].wait_recv()
        for side, way in enumerate(STEPS):
            for part in range(2):
                side_out[side, 2 * k, part] = edge_out[k, part, side] + edge_in[1 - k, part, side]
            corner = links.edge(side_out.at[side, 2 * k], side_in.at[side, 2 * k], "col", way)
            corner.start()
            sides.append(corner)
    summed.spread()
    for edge in inners + sides:
        edge.wait_recv()
    for k in range(3):
        at = k * n
        for part in range(2):
            ends = [side_out[side, k, part] + side_in[1 - side, k, part] for side in range(2)]
            if k == 1:
                mixed = jnp.where(upper, block(part, at, n), block(part, at, last - n))
                flat = grid[part, at : at + n, 2 * n : last - n]
            else:
                mixed = inner_out[k // 2, part, :, :n] + inner_in[1 - k // 2, part, :, :n]
                flat = inner_out[k // 2, part, :, n:] + inner_in[1 - k // 2, part, :, n:]

            def put(lo, hi, value):
                new_ext[part, at : at + n, lo:hi] = (
                    ext[part, at : at + n, lo:hi] - step_object * value
                )

            put(0, n, jnp.where(upper, ends[0], 0.0))
            put(n, 2 * n, jnp.where(upper, mixed, ends[0]))
            put(2 * n, last - n, flat)
            put(last - n, last, jnp.where(upper, ends[1], mixed))
            put(last, last + n, jnp.where(upper, 0.0, ends[1]))
    clear(links, "row", -1, new_ext.at[:, pl.ds(0, half), :])
    clear(links, "row", 1, new_ext.at[:, pl.ds(high - half, half), :])
    clear(links, "col", -1, new_ext.at[:, :, pl.ds(0, n)])
    clear(links, "col", 1, new_ext.at[:, :, pl.ds(last, n)])
    for edge in edges + inners + sides:
        edge.wait_send()
    summed.finish()


def final_kernel(
    sizes, scaling, ext, grid, probe, gradient, tile, new_probe,
    rim_out, rim_in, flat_in, mid_out, mid_in, end_out, end_in,
    shares, sums, total, send_sem, recv_sem,
):
    n = LANES
    half = n // 2
    high = ext.shape[1]
    last = ext.shape[2] - n
    tile_rows, tile_cols = tile.shape[1:]
    links = Links(sizes, send_sem, recv_sem)
    links.greet(True)
    summed = ProbeSum(links, scaling, probe, gradient, new_probe, shares, sums, total)
    upper = lax.broadcasted_iota(jnp.int32, (half, n), 1) >= half
    tall = lax.broadcasted_iota(jnp.int32, (n, n), 1) >= half
    outer = (0, high - half)
    inner = (half, high - n)
    rims = []
    flats = []
    for k, step in enumerate(STEPS):
        at = outer[k]
        for part in range(2):
            rim_out[k, part] = jnp.where(
                upper, grid[part, at : at + half, :n], grid[part, at : at + half, last:]
            )
        clear(links, "row", -step, rim_in.at[k])
        rim = links.edge(rim_out.at[k], rim_in.at[k], "row", step)
        rim.start()
        rims.append(rim)
        clear(links, "row", -step, flat_in.at[k])
        flats.append(
            links.edge(
                grid.at[:, pl.ds(at, half), pl.ds(n, tile_cols)], flat_in.at[k], "row", step
            )
        )

    def fuse(mask, side, real, imag):
        turned = pltpu.roll(imag, half, 1)
        return jnp.where(mask, real, turned) if side == 0 else jnp.where(mask, turned, real)

    middles = []
    for side, way in enumerate(STEPS):
        at = 0 if side == 0 else last
        mid_out[side] = fuse(
            tall, side, grid[0, n : high - n, at : at + n], grid[1, n : high - n, at : at + n]
        )
        clear(links, "col", -way, mid_in.at[side])
        clear(links, "col", -way, end_in.at[side])
        middle = links.edge(mid_out.at[side], mid_in.at[side], "col", way)
        middle.start()
        middles.append(middle)
    for flat in flats:
        flat.start()
    summed.across()
    for k in range(2):
        rims[1 - k].wait_recv()
        at = inner[k]
        for side, way in enumerate(STEPS):
            base = 0 if side == 0 else last
            values = [
                grid[part, at : at + half, base : base + n] + rim_in[1 - k, part]
                for part in range(2)
            ]
            end_out[side, k] = fuse(upper, side, values[0], values[1])
            end = links.edge(end_out.at[side, k], end_in.at[side, k], "col", way)
            end.start()
            middles.append(end)
    tile[:, half : tile_rows - half, :] = (
        ext[:, n : high - n, n:last] - step_object * grid[:, n : high - n, n:last]
    )
    summed.spread()
    for k in range(2):
        flats[1 - k].wait_recv()
        at = inner[k]
        tile[:, at - half : at, :] = ext[:, at : at + half, n:last] - step_object * (
            grid[:, at : at + half, n:last] + flat_in[1 - k]
        )
    for middle in middles:
        middle.wait_recv()

    def land(at, count, side, value, mask):
        base = tile_cols - n if side == 0 else 0
        keep = mask if side == 0 else jnp.logical_not(mask)
        turned = pltpu.roll(value, half, 1)
        for part, piece in enumerate((value, turned)):
            tile[part, at : at + count, base : base + n] -= step_object * jnp.where(
                keep, piece, 0.0
            )

    for side in range(2):
        land(half, n, side, mid_in[side], tall)
        for k in range(2):
            land(inner[k] - half, half, side, end_in[side, k], upper)
    for edge in rims + flats + middles:
        edge.wait_send()
    summed.finish()


def remote(kernel, collective_id, sizes, outs, scratch, copies, *operands):
    vmem = pl.BlockSpec(memory_space=pltpu.VMEM)
    return pl.pallas_call(
        kernel,
        out_shape=[jax.ShapeDtypeStruct(shape, jnp.float32) for shape in outs],
        in_specs=[vmem] * len(operands),
        out_specs=[vmem] * len(outs),
        scratch_shapes=[pltpu.VMEM(shape, jnp.float32) for shape in scratch]
        + [pltpu.SemaphoreType.DMA((copies,))] * 2,
        compiler_params=pltpu.CompilerParams(
            collective_id=collective_id,
            has_side_effects=True,
            vmem_limit_bytes=40 * 1024 * 1024,
        ),
    )(*operands)


def shards(object_field, probe_field, amplitudes, positions, counts):
    tile_rows = object_field.shape[1]
    tile_cols = object_field.shape[2]
    n = probe_field.shape[-1]
    half = n // 2
    slot_count = amplitudes.shape[2]
    sizes = {axis: lax.axis_size(axis) for axis in ("row", "col")}
    recorded = sizes["row"] * sizes["col"] * (2 * slot_count // 3)
    scaling = step_probe / recorded
    high_tables, low_tables = tables(n)
    measured = amplitudes[0, 0]
    wide = (2, tile_rows + n, tile_cols + 2 * n)
    share = 2 * n // sizes["row"]
    probe_scratch = [
        (sizes["row"] - 1, share, n), (sizes["col"], share, n), (8, n),
    ]
    probe_copies = 2 * (sizes["row"] - 1) + sizes["col"] - 1
    (extended,) = remote(
        functools.partial(halo_kernel, sizes), 0, sizes, [wide],
        [(2, tile_rows, n)] * 2 + [(2, 2, half, n)] * 2, 6, object_field,
    )
    for iteration in range(ITERS):
        grid, grad_probe = gradients(
            positions[0, 0], counts, extended, probe_field, measured,
            high_tables, low_tables,
        )
        operands = (
            extended, grid, probe_field.reshape(2 * n, n), grad_probe.reshape(2 * n, n)
        )
        if iteration < ITERS - 1:
            extended, probe_field = remote(
                functools.partial(middle_kernel, sizes, scaling), 1, sizes, [wide, (2 * n, n)],
                [(2, 2, 2, n, n)] * 2 + [(2, 2, n, tile_cols - n)] * 2 + [(2, 3, 2, n, n)] * 2
                + probe_scratch, 10 + probe_copies, *operands,
            )
        else:
            object_field, probe_field = remote(
                functools.partial(final_kernel, sizes, scaling), 2, sizes,
                [object_field.shape, (2 * n, n)],
                [(2, 2, half, n)] * 2 + [(2, 2, half, tile_cols)] + [(2, n, n)] * 2
                + [(2, 2, half, n)] * 2 + probe_scratch, 10 + probe_copies, *operands,
            )
        probe_field = probe_field.reshape(2, n, n)
    return (object_field, probe_field)


def solution(mesh):
    return jax.shard_map(
        shards,
        mesh=mesh,
        in_specs=(
            P(None, ("parts", "row"), "col"),
            P(),
            P("row", "col", "parts", None, None),
            P("row", "col", "parts", None),
            P(("parts", "row"), "col"),
        ),
        out_specs=(P(None, ("parts", "row"), "col"), P("parts", None, None)),
        check_vma=False,
    )
```

```python
import functools
import math

import jax
import jax.numpy as jnp
import numpy as np
from jax import lax
from jax.experimental import pallas as pl
from jax.experimental.pallas import tpu as pltpu
from jax.sharding import PartitionSpec as P

ITERS = 2


step_object = 0.25
step_probe = 0.5
floor_amp = 0.5
LANES = 128
GROUP = 4


def tables(size):
    index = np.arange(size)
    angle = 2.0 * math.pi / size * (index[:, None] * index[None, :] % size)
    scaling = 1.0 / math.sqrt(size)
    cosine, sine = (np.cos(angle) * scaling, np.sin(angle) * scaling)
    both = np.stack(
        [
            np.block([[cosine, -sine], [sine, cosine]]),
            np.block([[cosine, sine], [-sine, cosine]]),
        ]
    )
    high = both.astype(jnp.bfloat16)
    low = (both - high.astype(np.float64)).astype(jnp.bfloat16)
    return (jnp.asarray(high), jnp.asarray(low))


def split(value):
    high = value.astype(jnp.bfloat16)
    return high, (value - high.astype(jnp.float32)).astype(jnp.bfloat16)


def dot(a, b):
    return jnp.dot(a, b, preferred_element_type=jnp.float32)


def times_right(value, table_high, table_low):
    high, low = split(value)
    return dot(high, table_high) + dot(low, table_high) + dot(high, table_low)


def times_left(table_high, table_low, value):
    high, low = split(value)
    return dot(table_high, high) + dot(table_low, high) + dot(table_high, low)


def swap_blocks(value):
    n = LANES
    down, across = value.shape[0] // n, value.shape[1] // n
    return jnp.concatenate(
        [
            jnp.concatenate(
                [value[i * n : (i + 1) * n, j * n : (j + 1) * n] for i in range(down)], axis=1
            )
            for j in range(across)
        ],
        axis=0,
    )


def take_patch(source, part, place):
    n = LANES
    high_row, low_row, base, shift = place
    rows = n + 8
    lane = lax.broadcasted_iota(jnp.int32, (rows, n), 1)
    left = source[part, pl.ds(high_row, rows), pl.ds(base, n)]
    right = source[part, pl.ds(high_row, rows), pl.ds(base + n, n)]
    both = pltpu.roll(jnp.where(lane >= shift, left, right), (n - shift) % n, 1)
    turned = pltpu.roll(both.reshape(rows // 8, 8, n), (8 - low_row) % 8, 1)
    line = lax.broadcasted_iota(jnp.int32, (n // 8, 8, n), 1)
    return jnp.where(line < 8 - low_row, turned[:-1], turned[1:]).reshape(n, n)


def add_piece(grid, part, place, piece):
    n = LANES
    high_row, low_row, base, shift = place
    rows = n + 8
    turned = pltpu.roll(pltpu.roll(piece, shift, 1).reshape(n // 8, 8, n), low_row, 1)
    none = jnp.zeros((1, 8, n), jnp.float32)
    line = lax.broadcasted_iota(jnp.int32, (rows // 8, 8, n), 1)
    tall = jnp.where(
        line >= low_row,
        jnp.concatenate([turned, none], axis=0),
        jnp.concatenate([none, turned], axis=0),
    ).reshape(rows, n)
    lane = lax.broadcasted_iota(jnp.int32, (rows, n), 1)
    at_rows = pl.ds(high_row, rows)
    grid[part, at_rows, pl.ds(base, n)] += jnp.where(lane >= shift, tall, 0.0)
    grid[part, at_rows, pl.ds(base + n, n)] += jnp.where(lane >= shift, 0.0, tall)


def slots_kernel(
    centres, count, extended, probe, amplitude, high_tables, low_tables, grid, grad_probe
):
    n = LANES
    slot_count = amplitude.shape[0]
    grid[...] = jnp.zeros_like(grid)
    probe_real = probe[0]
    probe_imag = probe[1]
    probe_sum_real = jnp.zeros((n, n), jnp.float32)
    probe_sum_imag = jnp.zeros((n, n), jnp.float32)
    a_high, b_high = high_tables[0], high_tables[1]
    a_low, b_low = low_tables[0], low_tables[1]
    row_base = lax.axis_index("row") * (extended.shape[1] - n)
    col_base = lax.axis_index("col") * (extended.shape[2] - 2 * n) - n // 2
    for first in range(0, slot_count, GROUP):
        group = range(first, first + GROUP)
        patches = []
        exits = []
        places = []
        for slot in group:
            row_at = centres[0, slot] - row_base
            col_at = centres[1, slot] - col_base
            place = (
                pl.multiple_of(row_at // 8 * 8, 8),
                row_at % 8,
                pl.multiple_of(col_at // n * n, n),
                col_at % n,
            )
            patch = [take_patch(extended, part, place) for part in range(2)]
            patches.append(patch)
            places.append(place)
            exits.append(
                jnp.concatenate(
                    [
                        probe_real * patch[0] - probe_imag * patch[1],
                        probe_real * patch[1] + probe_imag * patch[0],
                    ],
                    axis=1,
                )
            )
        wave = times_right(jnp.concatenate(exits, axis=0), a_high, a_low)
        far = times_left(b_high, b_low, swap_blocks(wave))
        far_real, far_imag = far[:n], far[n:]
        measured = jnp.concatenate([amplitude[slot] for slot in group], axis=1)
        power = far_real * far_real + far_imag * far_imag
        keeping = 1.0 - measured * lax.rsqrt(jnp.maximum(power, floor_amp * floor_amp))
        kept = jnp.concatenate([far_real * keeping, far_imag * keeping], axis=0)
        back = times_left(a_high, a_low, kept)
        change = times_right(swap_blocks(back), b_high, b_low)
        for k, slot in enumerate(group):
            usable = jnp.where(slot < count[0, 0], 1.0, 0.0)
            change_real = change[k * n : (k + 1) * n, :n] * usable
            change_imag = change[k * n : (k + 1) * n, n:] * usable
            object_real, object_imag = patches[k]
            probe_sum_real += object_real * change_real + object_imag * change_imag
            probe_sum_imag += object_real * change_imag - object_imag * change_real
            pieces = (
                probe_real * change_real + probe_imag * change_imag,
                probe_real * change_imag - probe_imag * change_real,
            )
            for part in range(2):
                add_piece(grid, part, places[k], pieces[part])
    grad_probe[0] = probe_sum_real
    grad_probe[1] = probe_sum_imag


def gradients(centres, count, extended, probe, amplitude, high_tables, low_tables):
    smem = pl.BlockSpec(memory_space=pltpu.SMEM)
    vmem = pl.BlockSpec(memory_space=pltpu.VMEM)
    return pl.pallas_call(
        slots_kernel,
        out_shape=(
            jax.ShapeDtypeStruct(extended.shape, jnp.float32),
            jax.ShapeDtypeStruct(probe.shape, jnp.float32),
        ),
        in_specs=[smem] * 2 + [vmem] * 5,
        out_specs=(vmem, vmem),
        compiler_params=pltpu.CompilerParams(vmem_limit_bytes=40 * 1024 * 1024),
    )(centres, count, extended, probe, amplitude, high_tables, low_tables)


MESH = pl.DeviceIdType.MESH


class Links:
    def __init__(self, sizes, send_sem, recv_sem):
        self.sizes = sizes
        self.send_sem = send_sem
        self.recv_sem = recv_sem
        self.at = {axis: lax.axis_index(axis) for axis in sizes}
        self.used = 0

    def has(self, axis, step):
        return self.at[axis] > 0 if step < 0 else self.at[axis] < self.sizes[axis] - 1

    def peer(self, axis, step):
        size = self.sizes[axis]
        return lax.rem(self.at[axis] + (step + size), size)

    def greet(self, everyone):
        barrier = pltpu.get_barrier_semaphore()
        if everyone:
            for axis, size in self.sizes.items():
                for step in range(1, size):
                    pl.semaphore_signal(
                        barrier, inc=1, device_id={axis: self.peer(axis, step)}, device_id_type=MESH
                    )
            pl.semaphore_wait(barrier, sum(size - 1 for size in self.sizes.values()))
            return
        for axis in self.sizes:
            for step in (-1, 1):
                @pl.when(self.has(axis, step))
                def signal():
                    pl.semaphore_signal(
                        barrier, inc=1, device_id={axis: self.peer(axis, step)}, device_id_type=MESH
                    )
        peers = 0
        for axis in self.sizes:
            for step in (-1, 1):
                peers = peers + jnp.where(self.has(axis, step), 1, 0)
        pl.semaphore_wait(barrier, peers)

    def copy(self, src, dst, axis, step):
        number = self.used
        self.used += 1
        return pltpu.make_async_remote_copy(
            src_ref=src,
            dst_ref=dst,
            send_sem=self.send_sem.at[number],
            recv_sem=self.recv_sem.at[number],
            device_id={axis: self.peer(axis, step)},
            device_id_type=MESH,
        )

    def edge(self, src, dst, axis, step):
        return Edge(self, self.copy(src, dst, axis, step), axis, step)


class Edge:
    def __init__(self, links, copy, axis, step):
        self.links, self.copy, self.axis, self.step = links, copy, axis, step

    def start(self):
        pl.when(self.links.has(self.axis, self.step))(lambda: self.copy.start())

    def wait_send(self):
        pl.when(self.links.has(self.axis, self.step))(lambda: self.copy.wait_send())

    def wait_recv(self):
        pl.when(self.links.has(self.axis, -self.step))(lambda: self.copy.wait_recv())


def clear(links, axis, step, ref):
    @pl.when(jnp.logical_not(links.has(axis, step)))
    def fill():
        ref[...] = jnp.zeros(ref.shape, ref.dtype)


STEPS = (-1, 1)


def halo_kernel(sizes, tile, ext, band_out, band_in, corner_out, corner_in, send_sem, recv_sem, local_sem):
    n = LANES
    half = n // 2
    tile_rows, tile_cols = tile.shape[1:]
    last = tile_cols + n
    inside = pltpu.make_async_copy(
        tile, ext.at[:, pl.ds(half, tile_rows), pl.ds(n, tile_cols)], local_sem
    )
    inside.start()
    links = Links(sizes, send_sem, recv_sem)
    links.greet(False)
    inside.wait()
    rows = []
    for step in STEPS:
        src = ext.at[:, pl.ds(half if step < 0 else tile_rows, half), pl.ds(n, tile_cols)]
        to = tile_rows + half if step < 0 else 0
        rows.append(
            links.edge(src, ext.at[:, pl.ds(to, half), pl.ds(n, tile_cols)], "row", step)
        )
    lane = lax.broadcasted_iota(jnp.int32, (tile_rows, n), 1)
    bands = []
    for k, step in enumerate(STEPS):
        at = n if step < 0 else tile_cols
        real = ext[0, half : half + tile_rows, at : at + n]
        imag = pltpu.roll(ext[1, half : half + tile_rows, at : at + n], half, 1)
        low, high = (real, imag) if step < 0 else (imag, real)
        band_out[k] = jnp.where(lane < half, low, high)
        clear(links, "col", -step, band_in.at[k])
        band = links.edge(band_out.at[k], band_in.at[k], "col", step)
        band.start()
        bands.append(band)
    for row in rows:
        row.start()
    for k, step in enumerate(STEPS):
        clear(links, "row", -step, corner_in.at[k])
        to = tile_rows + half if step < 0 else 0
        clear(links, "row", -step, ext.at[:, pl.ds(to, half), pl.ds(n, tile_cols)])
    for k, step in enumerate(STEPS):
        bands[k].wait_recv()
        got = band_in[k]
        back = pltpu.roll(got, half, 1)
        at = last if step < 0 else 0
        keep = lane < half if step < 0 else lane >= half
        ext[0, half : half + tile_rows, at : at + n] = jnp.where(keep, got, 0.0)
        ext[1, half : half + tile_rows, at : at + n] = jnp.where(keep, back, 0.0)
    corners = []
    narrow = lax.broadcasted_iota(jnp.int32, (half, n), 1)
    for k, step in enumerate(STEPS):
        at = half if step < 0 else tile_rows
        for part in range(2):
            corner_out[k, part] = jnp.where(
                narrow >= half,
                ext[part, at : at + half, :n],
                ext[part, at : at + half, last : last + n],
            )
        corner = links.edge(corner_out.at[k], corner_in.at[k], "row", step)
        corner.start()
        corners.append(corner)
    for k, step in enumerate(STEPS):
        corners[k].wait_recv()
        to = tile_rows + half if step < 0 else 0
        for part in range(2):
            got = corner_in[k, part]
            ext[part, to : to + half, :n] = jnp.where(narrow >= half, got, 0.0)
            ext[part, to : to + half, last : last + n] = jnp.where(narrow < half, got, 0.0)
        rows[k].wait_recv()
    for edge in bands + rows + corners:
        edge.wait_send()


class ProbeSum:
    def __init__(self, links, scaling, probe, gradient, new_probe, shares, sums, total):
        self.links, self.scaling = links, scaling
        self.probe, self.new_probe = probe, new_probe
        self.shares, self.sums, self.total = shares, sums, total
        self.count = gradient.shape[0] // links.sizes["row"]
        self.mine = self.share(links.at["row"])
        self.gradient = gradient
        self.copies = []
        self.first = []
        for step in range(1, links.sizes["row"]):
            src = gradient.at[self.share(links.peer("row", step)), :]
            self.first.append(links.copy(src, shares.at[step - 1], "row", step))
        for copy in self.first:
            copy.start()

    def share(self, owner):
        return pl.ds(pl.multiple_of(owner * self.count, self.count), self.count)

    def across(self):
        links = self.links
        value = self.gradient[self.mine, :]
        for k, copy in enumerate(self.first):
            copy.wait_recv()
            value = value + self.shares[k]
        own = links.at["col"]
        self.sums[own] = value
        self.second = []
        for step in range(1, links.sizes["col"]):
            self.second.append(links.copy(self.sums.at[own], self.sums.at[own], "col", step))
        for copy in self.second:
            copy.start()

    def spread(self):
        links = self.links
        for copy in self.second:
            copy.wait_recv()
        value = self.sums[0]
        for k in range(1, links.sizes["col"]):
            value = value + self.sums[k]
        self.new_probe[self.mine, :] = self.probe[self.mine, :] - self.scaling * value
        self.third = []
        for step in range(1, links.sizes["row"]):
            ref = self.new_probe.at[self.mine, :]
            self.third.append(links.copy(ref, ref, "row", step))
        for copy in self.third:
            copy.start()

    def finish(self):
        for copy in self.third:
            copy.wait_recv()
        for copy in self.first + self.second + self.third:
            copy.wait_send()


def middle_kernel(
    sizes, scaling, ext, grid, probe, gradient, new_ext, new_probe,
    edge_out, edge_in, inner_out, inner_in, side_out, side_in,
    shares, sums, total, send_sem, recv_sem,
):
    n = LANES
    half = n // 2
    high = ext.shape[1]
    last = ext.shape[2] - n
    links = Links(sizes, send_sem, recv_sem)
    links.greet(True)
    summed = ProbeSum(links, scaling, probe, gradient, new_probe, shares, sums, total)
    upper = lax.broadcasted_iota(jnp.int32, (n, n), 1) >= half

    def block(part, at, k):
        return grid[part, at : at + n, k : k + n]

    def band(part, at, side):
        base = 0 if side == 0 else last - n
        return jnp.where(upper, block(part, at, base), block(part, at, base + n))

    tops = (0, high - n)
    edges = []
    for k, step in enumerate(STEPS):
        for part in range(2):
            for side in range(2):
                edge_out[k, part, side] = band(part, tops[k], side)
        clear(links, "row", -step, edge_in.at[k])
        edge = links.edge(edge_out.at[k], edge_in.at[k], "row", step)
        edge.start()
        edges.append(edge)
    sides = []
    for k, step in enumerate(STEPS):
        for part in range(2):
            side_out[k, 1, part] = band(part, n, k)
        clear(links, "col", -step, side_in.at[k])
        side = links.edge(side_out.at[k, 1], side_in.at[k, 1], "col", step)
        side.start()
        sides.append(side)
    inners = []
    for k, step in enumerate(STEPS):
        for part in range(2):
            inner_out[k, part, :, :n] = jnp.where(
                upper, block(part, tops[k], n), block(part, tops[k], last - n)
            )
            inner_out[k, part, :, n:] = grid[part, tops[k] : tops[k] + n, 2 * n : last - n]
        clear(links, "row", -step, inner_in.at[k])
        inner = links.edge(inner_out.at[k], inner_in.at[k], "row", step)
        inner.start()
        inners.append(inner)
    summed.across()
    for k, step in enumerate(STEPS):
        edges[1 - k].wait_recv()
        for side, way in enumerate(STEPS):
            for part in range(2):
                side_out[side, 2 * k, part] = edge_out[k, part, side] + edge_in[1 - k, part, side]
            corner = links.edge(side_out.at[side, 2 * k], side_in.at[side, 2 * k], "col", way)
            corner.start()
            sides.append(corner)
    summed.spread()
    for edge in inners + sides:
        edge.wait_recv()
    for k in range(3):
        at = k * n
        for part in range(2):
            ends = [side_out[side, k, part] + side_in[1 - side, k, part] for side in range(2)]
            if k == 1:
                mixed = jnp.where(upper, block(part, at, n), block(part, at, last - n))
                flat = grid[part, at : at + n, 2 * n : last - n]
            else:
                mixed = inner_out[k // 2, part, :, :n] + inner_in[1 - k // 2, part, :, :n]
                flat = inner_out[k // 2, part, :, n:] + inner_in[1 - k // 2, part, :, n:]

            def put(lo, hi, value):
                new_ext[part, at : at + n, lo:hi] = (
                    ext[part, at : at + n, lo:hi] - step_object * value
                )

            put(0, n, jnp.where(upper, ends[0], 0.0))
            put(n, 2 * n, jnp.where(upper, mixed, ends[0]))
            put(2 * n, last - n, flat)
            put(last - n, last, jnp.where(upper, ends[1], mixed))
            put(last, last + n, jnp.where(upper, 0.0, ends[1]))
    clear(links, "row", -1, new_ext.at[:, pl.ds(0, half), :])
    clear(links, "row", 1, new_ext.at[:, pl.ds(high - half, half), :])
    clear(links, "col", -1, new_ext.at[:, :, pl.ds(0, n)])
    clear(links, "col", 1, new_ext.at[:, :, pl.ds(last, n)])
    for edge in edges + inners + sides:
        edge.wait_send()
    summed.finish()


def final_kernel(
    sizes, scaling, ext, grid, probe, gradient, tile, new_probe,
    rim_out, rim_in, flat_in, mid_out, mid_in, end_out, end_in,
    shares, sums, total, send_sem, recv_sem,
):
    n = LANES
    half = n // 2
    high = ext.shape[1]
    last = ext.shape[2] - n
    tile_rows, tile_cols = tile.shape[1:]
    links = Links(sizes, send_sem, recv_sem)
    links.greet(True)
    summed = ProbeSum(links, scaling, probe, gradient, new_probe, shares, sums, total)
    upper = lax.broadcasted_iota(jnp.int32, (half, n), 1) >= half
    tall = lax.broadcasted_iota(jnp.int32, (n, n), 1) >= half
    outer = (0, high - half)
    inner = (half, high - n)
    rims = []
    flats = []
    for k, step in enumerate(STEPS):
        at = outer[k]
        for part in range(2):
            rim_out[k, part] = jnp.where(
                upper, grid[part, at : at + half, :n], grid[part, at : at + half, last:]
            )
        clear(links, "row", -step, rim_in.at[k])
        rim = links.edge(rim_out.at[k], rim_in.at[k], "row", step)
        rim.start()
        rims.append(rim)
        clear(links, "row", -step, flat_in.at[k])
        flats.append(
            links.edge(
                grid.at[:, pl.ds(at, half), pl.ds(n, tile_cols)], flat_in.at[k], "row", step
            )
        )

    def fuse(mask, side, real, imag):
        turned = pltpu.roll(imag, half, 1)
        return jnp.where(mask, real, turned) if side == 0 else jnp.where(mask, turned, real)

    middles = []
    for side, way in enumerate(STEPS):
        at = 0 if side == 0 else last
        mid_out[side] = fuse(
            tall, side, grid[0, n : high - n, at : at + n], grid[1, n : high - n, at : at + n]
        )
        clear(links, "col", -way, mid_in.at[side])
        clear(links, "col", -way, end_in.at[side])
        middle = links.edge(mid_out.at[side], mid_in.at[side], "col", way)
        middle.start()
        middles.append(middle)
    for flat in flats:
        flat.start()
    summed.across()
    for k in range(2):
        rims[1 - k].wait_recv()
        at = inner[k]
        for side, way in enumerate(STEPS):
            base = 0 if side == 0 else last
            values = [
                grid[part, at : at + half, base : base + n] + rim_in[1 - k, part]
                for part in range(2)
            ]
            end_out[side, k] = fuse(upper, side, values[0], values[1])
            end = links.edge(end_out.at[side, k], end_in.at[side, k], "col", way)
            end.start()
            middles.append(end)
    tile[:, half : tile_rows - half, :] = (
        ext[:, n : high - n, n:last] - step_object * grid[:, n : high - n, n:last]
    )
    summed.spread()
    for k in range(2):
        flats[1 - k].wait_recv()
        at = inner[k]
        tile[:, at - half : at, :] = ext[:, at : at + half, n:last] - step_object * (
            grid[:, at : at + half, n:last] + flat_in[1 - k]
        )
    for middle in middles:
        middle.wait_recv()

    def land(at, count, side, value, mask):
        base = tile_cols - n if side == 0 else 0
        keep = mask if side == 0 else jnp.logical_not(mask)
        turned = pltpu.roll(value, half, 1)
        for part, piece in enumerate((value, turned)):
            tile[part, at : at + count, base : base + n] -= step_object * jnp.where(
                keep, piece, 0.0
            )

    for side in range(2):
        land(half, n, side, mid_in[side], tall)
        for k in range(2):
            land(inner[k] - half, half, side, end_in[side, k], upper)
    for edge in rims + flats + middles:
        edge.wait_send()
    summed.finish()


def remote(kernel, collective_id, sizes, outs, scratch, copies, *operands, place=pltpu.VMEM, more=()):
    vmem = pl.BlockSpec(memory_space=pltpu.VMEM)
    return pl.pallas_call(
        kernel,
        out_shape=[jax.ShapeDtypeStruct(shape, jnp.float32) for shape in outs],
        in_specs=[pl.BlockSpec(memory_space=place)] * len(operands),
        out_specs=[vmem] * len(outs),
        scratch_shapes=[pltpu.VMEM(shape, jnp.float32) for shape in scratch]
        + [pltpu.SemaphoreType.DMA((copies,))] * 2
        + list(more),
        compiler_params=pltpu.CompilerParams(
            collective_id=collective_id,
            has_side_effects=True,
            vmem_limit_bytes=40 * 1024 * 1024,
        ),
    )(*operands)


def shards(object_field, probe_field, amplitudes, positions, counts):
    tile_rows = object_field.shape[1]
    tile_cols = object_field.shape[2]
    n = probe_field.shape[-1]
    half = n // 2
    slot_count = amplitudes.shape[2]
    sizes = {axis: lax.axis_size(axis) for axis in ("row", "col")}
    recorded = sizes["row"] * sizes["col"] * (2 * slot_count // 3)
    scaling = step_probe / recorded
    high_tables, low_tables = tables(n)
    measured = amplitudes[0, 0]
    wide = (2, tile_rows + n, tile_cols + 2 * n)
    share = 2 * n // sizes["row"]
    probe_scratch = [
        (sizes["row"] - 1, share, n), (sizes["col"], share, n), (8, n),
    ]
    probe_copies = 2 * (sizes["row"] - 1) + sizes["col"] - 1
    (extended,) = remote(
        functools.partial(halo_kernel, sizes), 0, sizes, [wide],
        [(2, tile_rows, n)] * 2 + [(2, 2, half, n)] * 2, 6, object_field,
        place=pltpu.HBM, more=(pltpu.SemaphoreType.DMA,),
    )
    for iteration in range(ITERS):
        grid, grad_probe = gradients(
            positions[0, 0], counts, extended, probe_field, measured,
            high_tables, low_tables,
        )
        operands = (
            extended, grid, probe_field.reshape(2 * n, n), grad_probe.reshape(2 * n, n)
        )
        if iteration < ITERS - 1:
            extended, probe_field = remote(
                functools.partial(middle_kernel, sizes, scaling), 1, sizes, [wide, (2 * n, n)],
                [(2, 2, 2, n, n)] * 2 + [(2, 2, n, tile_cols - n)] * 2 + [(2, 3, 2, n, n)] * 2
                + probe_scratch, 10 + probe_copies, *operands,
            )
        else:
            object_field, probe_field = remote(
                functools.partial(final_kernel, sizes, scaling), 2, sizes,
                [object_field.shape, (2 * n, n)],
                [(2, 2, half, n)] * 2 + [(2, 2, half, tile_cols)] + [(2, n, n)] * 2
                + [(2, 2, half, n)] * 2 + probe_scratch, 10 + probe_copies, *operands,
            )
        probe_field = probe_field.reshape(2, n, n)
    return (object_field, probe_field)


def solution(mesh):
    return jax.shard_map(
        shards,
        mesh=mesh,
        in_specs=(
            P(None, ("parts", "row"), "col"),
            P(),
            P("row", "col", "parts", None, None),
            P("row", "col", "parts", None),
            P(("parts", "row"), "col"),
        ),
        out_specs=(P(None, ("parts", "row"), "col"), P("parts", None, None)),
        check_vma=False,
    )
```
